32 devices in a mesh: ctx: 8 (over y, x, core), head: 4 (over z).
Axes of the slice: x: 2, y: 2, z: 4, core: 2. Of those that a mesh axis runs over, the one named last changes fastest.
Arguments:
- queries: bfloat16 [8192, 4096], P('ctx', 'head'), may hold values from -100 to 100
- keys: bfloat16 [8192, 4096], P('ctx', 'head'), may hold values from -5 to 5
- values: bfloat16 [8192, 4096], P('ctx', 'head'), may hold values from -12 to 12
- block_perm: int32 [32, 32], P('head'), may hold values from 0 to 31, as said below
- norm_gain: float32 [4096], P('head'), may hold values from 0.5 to 1.5
Outputs:
- normalized: bfloat16 [8192, 4096], P('ctx', 'head')
The draws below stay inside these ranges and needn't reach their ends.
Inputs may be any that keep to these rules, and one draw needn't show every extreme that they name: `block_perm`: each row is a permutation of the 32 blocks. With the blocks of one index of ctx being 4 consecutive blocks: in one head, at most one query block of one ctx index matches a key block of one given ctx index; over the 8 consecutive heads of one head group, at most 4 do, and some pairs of ctx indices reach 4 in every group.
All inputs are finite; a program needn't handle non-finite values.
Results may differ from the reference program's by a relative error of at most 0.0046.
Values may be sent and summed in bfloat16 or wider, within the bound.
No kernel may reach another device: no remote copies, remote signals or barrier semaphores. Data moves between devices by JAX's collectives and lax.ppermute only.
A program may use at most 128 MiB of HBM per device.

```python
import math
from functools import partial
import jax
import jax.numpy as jnp
from jax import lax

HEADS = 32
HD = 128
BLOCK = 256
BLK_DEV = 4
HEADS_DEV = 8
NBLOCKS = 32
TOKENS = 8192
D = 4096


def shared_rows(key):
    return jnp.clip(jax.random.normal(key, (TOKENS, D), jnp.float32), -5.0, 5.0)


def draw_queries(key, part):
    key = jax.random.fold_in(key, 1)
    result = jnp.clip(jax.random.normal(key, (TOKENS, D), jnp.float32), -5.0, 5.0)
    return result.astype(jnp.bfloat16)


def draw_keys(key, part):
    base_rows = shared_rows(key)
    result = base_rows
    return result.astype(jnp.bfloat16)


def draw_values(key, part):
    key = jax.random.fold_in(key, 3)
    columns = (jnp.arange(D, dtype=jnp.int32) // HD).astype(jnp.float32)
    spread = 3.0 ** (0.5 * columns / (HEADS - 1))
    base_vals = jnp.clip(jax.random.normal(key, (TOKENS, D), jnp.float32), -4.0, 4.0)
    return (base_vals * spread[None, :]).astype(jnp.bfloat16)


def shuffles(base_key, how_many, length):
    return jax.vmap(lambda one_key: jax.random.permutation(one_key, length))(jax.random.split(base_key, how_many)).astype(jnp.int32)


def draw_block_perm(key, part):
    key = jax.random.fold_in(key, 4)
    ctx_count = NBLOCKS // BLK_DEV
    group_count = HEADS // HEADS_DEV
    pair_count = HEADS_DEV // 2
    key_outer, key_inner, key_within, key_local = jax.random.split(key, 4)
    outer_perm = shuffles(key_outer, group_count, ctx_count)
    inner_perm = shuffles(key_inner, group_count, ctx_count)
    within = shuffles(key_within, group_count * pair_count, BLK_DEV).reshape(group_count, pair_count, BLK_DEV)
    local_order = shuffles(key_local, HEADS * ctx_count, BLK_DEV).reshape(HEADS, ctx_count * BLK_DEV)
    heads_all = jnp.arange(HEADS, dtype=jnp.int32)
    group_of = heads_all // HEADS_DEV
    pair_of = heads_all % HEADS_DEV // 2
    offsets = (within[group_of, pair_of] + BLK_DEV * pair_of[:, None]) % ctx_count
    spot_ids = (inner_perm[group_of][:, :, None] + offsets[:, None, :]) % ctx_count
    source_dev = jnp.take_along_axis(outer_perm[group_of], spot_ids.reshape(HEADS, ctx_count * BLK_DEV), axis=1)
    slot_j = jnp.tile(jnp.arange(BLK_DEV, dtype=jnp.int32), ctx_count)
    local_ids = jnp.take_along_axis(local_order, source_dev * BLK_DEV + slot_j[None, :], axis=1)
    return (source_dev * BLK_DEV + local_ids).astype(jnp.int32)


def setup_inputs(seed: int = 0) -> dict:
    arg_keys = jax.random.split(jax.random.key(seed), 6)
    return {
        "queries": draw_queries(jax.random.fold_in(arg_keys[5], 71), 0),
        "keys": draw_keys(jax.random.fold_in(arg_keys[5], 71), 0),
        "values": draw_values(jax.random.fold_in(arg_keys[5], 71), 0),
        "block_perm": draw_block_perm(jax.random.fold_in(arg_keys[5], 71), 0),
        "norm_gain": jnp.clip(1.0 + 0.1 * jax.random.normal(arg_keys[4], (D,), jnp.float32), 0.5, 1.5),
    }


NORM_EPS = 1e-06

def rounded_output(weights):
    return lax.optimization_barrier(weights.astype(jnp.bfloat16)).astype(jnp.float32)

def attend_head(queries, keys, values, block_perm, head_index):
    col_start = head_index * HD

    def to_tiles(array):
        piece = lax.dynamic_slice_in_dim(array, col_start, HD, 1)
        return piece.astype(jnp.float32).reshape(NBLOCKS, BLOCK, HD)
    query_tiles = to_tiles(queries)
    key_tiles = to_tiles(keys)
    value_block_grid = to_tiles(values)
    zero_tile = jnp.zeros((1, BLOCK, HD), jnp.float32)
    prev_keys = jnp.concatenate([zero_tile, key_tiles[:-1]], axis=0)
    previous_block_values = jnp.concatenate([zero_tile, value_block_grid[:-1]], axis=0)
    perm_row = lax.dynamic_index_in_dim(block_perm, head_index, 0, keepdims=False)
    matched_keys = jnp.take(key_tiles, perm_row, axis=0)
    sorted_block_values = jnp.take(value_block_grid, perm_row, axis=0)
    logit_scale_factor = 1.0 / math.sqrt(HD)

    def scores(left_operand, right_operand):
        return jnp.einsum('oiu,ozu->oiz', left_operand, right_operand) * logit_scale_factor
    causal = jnp.arange(BLOCK)[:, None] >= jnp.arange(BLOCK)[None, :]
    block_ids = jnp.arange(NBLOCKS)
    own_scores = jnp.where(causal[None], scores(query_tiles, key_tiles), -jnp.inf)
    prev_scores = jnp.where((block_ids > 0)[:, None, None], scores(query_tiles, prev_keys), -jnp.inf)
    match_scores = scores(query_tiles, matched_keys)
    row_max = jnp.maximum(jnp.maximum(lax.optimization_barrier(jnp.max(own_scores, axis=-1)), lax.optimization_barrier(jnp.max(prev_scores, axis=-1))), lax.optimization_barrier(jnp.max(match_scores, axis=-1)))[..., None]
    local_block_weights = jnp.exp(own_scores - row_max)
    previous_block_weights = jnp.exp(prev_scores - row_max)
    matched_block_weights = jnp.exp(match_scores - row_max)
    weight_sum = lax.optimization_barrier(jnp.sum(local_block_weights, axis=-1)) + lax.optimization_barrier(jnp.sum(previous_block_weights, axis=-1)) + lax.optimization_barrier(jnp.sum(matched_block_weights, axis=-1))
    blended_output = jnp.einsum('elz,ezc->elc', rounded_output(local_block_weights), value_block_grid)
    blended_output = blended_output + jnp.einsum('elz,ezc->elc', rounded_output(previous_block_weights), previous_block_values)
    blended_output = blended_output + jnp.einsum('elz,ezc->elc', rounded_output(matched_block_weights), sorted_block_values)
    return blended_output / weight_sum[..., None]

def reference(queries, keys, values, block_perm, norm_gain):
    head_outputs = lax.map(partial(attend_head, queries, keys, values, block_perm), jnp.arange(HEADS, dtype=jnp.int32))
    attended = head_outputs.transpose(1, 2, 0, 3).reshape(TOKENS, D)
    mean_square = lax.optimization_barrier(jnp.sum(attended * attended, axis=1)) / D
    inverse = lax.rsqrt(mean_square + NORM_EPS)
    return (attended * inverse[:, None] * norm_gain[None, :]).astype(jnp.bfloat16)
```

```python
import functools
import math

import jax
import jax.numpy as jnp
from jax import lax
from jax.experimental import pallas as pl
from jax.experimental.pallas import tpu as pltpu
from jax.sharding import PartitionSpec as P

NORM_EPS = 1e-06
VMEM_LIMIT = 24 * 1024 * 1024
ANY = pl.BlockSpec(memory_space=pl.ANY)
SMEM = pl.BlockSpec(memory_space=pltpu.SMEM)
VMEM = pl.BlockSpec(memory_space=pltpu.VMEM)
PARAMS = pltpu.CompilerParams(vmem_limit_bytes=VMEM_LIMIT)
CONTRACT_LAST = (((1,), (1,)), ((), ()))


def near(array):
    return pltpu.with_memory_space_constraint(array, pltpu.VMEM)


def tile(block, head, block_len, head_dim):
    rows = pl.ds(pl.multiple_of(block * block_len, block_len), block_len)
    return rows, pl.ds(pl.multiple_of(head * head_dim, head_dim), head_dim)


def last_kernel(block_len, keys, values, out, sems):
    rows = pl.ds(keys.shape[0] - block_len, block_len)
    copies = [
        pltpu.make_async_copy(array.at[rows], out.at[i], sems.at[i])
        for i, array in enumerate((keys, values))
    ]
    for copy in copies:
        copy.start()
    for copy in copies:
        copy.wait()


def last_blocks(keys, values, block_len):
    return pl.pallas_call(
        functools.partial(last_kernel, block_len),
        out_shape=pltpu.VMEM((2, block_len, keys.shape[1]), keys.dtype),
        in_specs=[ANY, ANY],
        out_specs=VMEM,
        scratch_shapes=[pltpu.SemaphoreType.DMA((2,))],
        compiler_params=PARAMS,
        name="last_blocks",
    )(keys, values)


def pack_kernel(sizes, partners, listing, rank_ref, perm_ref, keys, values, *rest):
    ctx_size, blocks, head_count, capacity, block_len, head_dim, _ = sizes
    sends, rest = rest[: len(partners)], rest[len(partners) :]
    if listing:
        table, rest = rest[0], rest[1:]
    counts, sems = rest
    rank = rank_ref[0]
    full = ctx_size * capacity == head_count * blocks

    def copies(i, slot, block, head):
        for which, array in enumerate((keys, values)):
            yield pltpu.make_async_copy(
                array.at[tile(block, head, block_len, head_dim)],
                sends[i].at[which, slot],
                sems.at[i, slot, which],
            )

    for i, d in enumerate(partners):
        other = jnp.bitwise_xor(rank, d)
        counts[i] = 0
        for head in range(head_count):
            found = jnp.int32(-1)
            for j in range(blocks):
                source = perm_ref[head, other * blocks + j] - rank * blocks
                found = jnp.where((source >= 0) & (source < blocks), source, found)
            slot = counts[i]

            @pl.when(found >= 0)
            def _():
                for copy in copies(i, slot, found, head):
                    copy.start()
                counts[i] = slot + 1

    if listing:
        for d in range(ctx_size):
            if not full:
                for slot in range(capacity):
                    table[d * capacity + slot] = -1
            other = jnp.bitwise_xor(rank, d)
            place = jnp.int32(0)
            for head in range(head_count):
                item = jnp.int32(-1)
                for j in range(blocks):
                    source = perm_ref[head, rank * blocks + j] - other * blocks
                    hit = (source >= 0) & (source < blocks)
                    item = jnp.where(hit, (head * blocks + j) * blocks + source, item)

                @pl.when(item >= 0)
                def _():
                    table[d * capacity + place] = item

                place = place + (item >= 0).astype(jnp.int32)

    for i in range(len(partners)):
        for slot in range(capacity):

            @pl.when(slot < counts[i])
            def _():
                for copy in copies(i, slot, 0, 0):
                    copy.wait()


def pack(sizes, partners, listing, rank, perm, keys, values):
    ctx_size, blocks, head_count, capacity, block_len, head_dim, _ = sizes
    out_shape = [
        pltpu.VMEM((2, capacity, block_len, head_dim), keys.dtype) for d in partners
    ]
    out_specs = [VMEM] * len(partners)
    if listing:
        out_shape.append(jax.ShapeDtypeStruct((ctx_size * capacity,), jnp.int32))
        out_specs.append(SMEM)
    moved = 8 * len(partners) * capacity * block_len * head_dim
    return pl.pallas_call(
        functools.partial(pack_kernel, sizes, partners, listing),
        out_shape=out_shape,
        in_specs=[SMEM, SMEM, ANY, ANY],
        out_specs=out_specs,
        scratch_shapes=[
            pltpu.SMEM((len(partners),), jnp.int32),
            pltpu.SemaphoreType.DMA((len(partners), capacity, 2)),
        ],
        compiler_params=PARAMS,
        cost_estimate=pl.CostEstimate(flops=0, bytes_accessed=moved, transcendentals=0),
        name="pack_tiles",
    )(rank, perm, keys, values)


def attend_kernel(sizes, group, first, rank_ref, table, queries, keys, values, prev, *rest):
    ctx_size, blocks, head_count, capacity, block_len, head_dim, scale = sizes
    remote = [d for d in group if d > 0]
    received, rest = rest[: len(remote)], rest[len(remote) :]
    attended, squares = rest[-2:]
    if first:
        squares[...] = jnp.zeros_like(squares)
    rank = rank_ref[0]
    full = ctx_size * capacity == head_count * blocks
    ones = jnp.ones((block_len, head_dim), jnp.bfloat16)

    def work(d, c, item):
        source = lax.rem(item, blocks)
        block = lax.rem(lax.div(item, blocks), blocks)
        head = lax.div(item, blocks * blocks)
        here = tile(block, head, block_len, head_dim)
        before = tile(jnp.maximum(block - 1, 0), head, block_len, head_dim)
        inside = block > 0
        if d > 0:
            match = [received[remote.index(d)][i, c] for i in range(2)]
        else:
            match = [array[tile(source, head, block_len, head_dim)] for array in (keys, values)]
        previous = [
            jnp.where(inside, array[before], prev[i, :, here[1]])
            for i, array in enumerate((keys, values))
        ]
        own = [keys[here], values[here]]
        q = queries[here]
        has_prev = rank * blocks + block > 0
        scores = [
            lax.dot_general(q, k, CONTRACT_LAST, preferred_element_type=jnp.float32)
            for k, _ in (own, previous, match)
        ]
        row = lax.broadcasted_iota(jnp.int32, (block_len, block_len), 0)
        column = lax.broadcasted_iota(jnp.int32, (block_len, block_len), 1)
        scores[0] = jnp.where(row >= column, scores[0], -jnp.inf)
        peak = jnp.max(jnp.maximum(scores[0], scores[2]), axis=1, keepdims=True)
        prev_peak = jnp.max(scores[1], axis=1, keepdims=True)
        peak = jnp.maximum(peak, jnp.where(has_prev, prev_peak, -jnp.inf))
        shifts = (peak, jnp.where(has_prev, peak, jnp.inf), peak)
        total = None
        for score, shift, (_, v) in zip(scores, shifts, (own, previous, match)):
            weights = jnp.exp2((score - shift) * (scale * math.log2(math.e)))
            part = jnp.dot(
                weights.astype(jnp.bfloat16),
                jnp.concatenate([v, ones], axis=1),
                preferred_element_type=jnp.float32,
            )
            total = part if total is None else total + part
        result = total[:, :head_dim] / total[:, head_dim:]
        attended[here] = result
        squares[here[0]] += result * result

    for d in group:
        for c in range(capacity):
            item = table[d * capacity + c]
            if full:
                work(d, c, item)
            else:
                pl.when(item >= 0)(functools.partial(work, d, c, item))


def attend(sizes, group, state, rank, table, queries, keys, values, prev, received):
    ctx_size, blocks, head_count, capacity, block_len, head_dim, _ = sizes
    first = state is None
    count = len(group) * capacity
    tok_rows, row_width = queries.shape
    arrays = [queries, keys, values, prev] + [received[d] for d in group if d > 0]
    aliases = {}
    if not first:
        aliases = {len(arrays) + 2: 0, len(arrays) + 3: 1}
        arrays += list(state)
    return pl.pallas_call(
        functools.partial(attend_kernel, sizes, group, first),
        out_shape=[
            pltpu.VMEM((tok_rows, row_width), jnp.float32),
            pltpu.VMEM((tok_rows, head_dim), jnp.float32),
        ],
        in_specs=[SMEM, SMEM] + [VMEM] * len(arrays),
        out_specs=[VMEM, VMEM],
        input_output_aliases=aliases,
        compiler_params=PARAMS,
        cost_estimate=pl.CostEstimate(
            flops=count * 24 * block_len * block_len * head_dim,
            bytes_accessed=count * block_len * head_dim * 18,
            transcendentals=count * 3 * block_len * block_len,
        ),
        name="attend_items",
    )(rank, table, *[near(array) for array in arrays])


def total_kernel(squares, out):
    out[...] = lax.dot_general(
        jnp.ones((8, squares.shape[1]), jnp.float32),
        squares[...],
        CONTRACT_LAST,
        precision=lax.Precision.HIGHEST,
        preferred_element_type=jnp.float32,
    )[:1]


def totals(squares):
    return pl.pallas_call(
        total_kernel,
        out_shape=jax.ShapeDtypeStruct((1, squares.shape[0]), jnp.float32),
        in_specs=[VMEM],
        out_specs=VMEM,
        compiler_params=PARAMS,
        name="row_totals",
    )(near(squares))


def scale_kernel(width, block_len, gain, *rest):
    sums, (attended, out, buffer, sems) = rest[:-4], rest[-4:]
    total = sums[0][...]
    for other in sums[1:]:
        total = total + other[...]
    inverse = lax.rsqrt(total / width + NORM_EPS)
    steps = attended.shape[0] // block_len
    copies = []
    for i in range(steps):
        rows = slice(i * block_len, (i + 1) * block_len)
        column = jnp.transpose(jnp.broadcast_to(inverse[:, rows], (8, block_len)))[:, :1]
        buffer[rows] = (attended[rows] * column * gain[...]).astype(out.dtype)
        copies.append(pltpu.make_async_copy(buffer.at[rows], out.at[rows], sems.at[i]))
        copies[i].start()
    for copy in copies:
        copy.wait()


def scaled(attended, sums, gain, width, block_len):
    tok_rows, row_width = attended.shape
    return pl.pallas_call(
        functools.partial(scale_kernel, width, block_len),
        out_shape=jax.ShapeDtypeStruct((tok_rows, row_width), jnp.bfloat16),
        in_specs=[VMEM] * (len(sums) + 2),
        out_specs=ANY,
        scratch_shapes=[
            pltpu.VMEM((tok_rows, row_width), jnp.bfloat16),
            pltpu.SemaphoreType.DMA((tok_rows // block_len,)),
        ],
        compiler_params=PARAMS,
        name="scale_rows",
    )(gain.reshape(1, row_width), *sums, near(attended))


def per_device(queries, keys, values, block_perm, norm_gain):
    ctx_size = lax.axis_size("ctx")
    head_size = lax.axis_size("head")
    head_count = block_perm.shape[0]
    blocks = block_perm.shape[1] // ctx_size
    tok_rows, row_width = queries.shape
    block_len = tok_rows // blocks
    head_dim = row_width // head_count
    capacity = head_count // 2
    sizes = (
        ctx_size, blocks, head_count, capacity, block_len, head_dim, 1.0 / math.sqrt(head_dim)
    )
    rank = lax.axis_index("ctx").astype(jnp.int32).reshape(1)

    last = last_blocks(keys, values, block_len)
    prev = lax.ppermute(last, "ctx", [(i, i + 1) for i in range(ctx_size - 1)])
    order = sorted(range(1, ctx_size), key=ORDER.index) if ctx_size == len(ORDER) + 1 else list(range(ctx_size - 1, 0, -1))
    *sends, table = pack(sizes, order, True, rank, block_perm, keys, values)
    received = {}
    for d, send in zip(order, sends):
        received[d] = lax.ppermute(send, "ctx", [(i, i ^ d) for i in range(ctx_size)])
    state = None
    for d in [0] + order:
        state = attend(
            sizes, (d,), state, rank, table, queries, keys, values, prev, received
        )
    attended, squares = state
    sums = [totals(squares)]
    for d in range(1, head_size):
        sums.append(lax.ppermute(sums[0], "head", [(i, i ^ d) for i in range(head_size)]))
    return scaled(attended, sums, norm_gain, row_width * head_size, block_len)


ORDER = [1, 6, 4, 7, 5, 2, 3]


def solution(mesh):
    placed = (P("ctx", "head"), P("ctx", "head"), P("ctx", "head"), P("head", None), P("head"))
    return jax.shard_map(
        per_device, mesh=mesh, in_specs=placed, out_specs=P("ctx", "head"), check_vma=False
    )
```

```python
import functools
import math

import jax
import jax.numpy as jnp
from jax import lax
from jax.experimental import pallas as pl
from jax.experimental.pallas import tpu as pltpu
from jax.sharding import PartitionSpec as P

NORM_EPS = 1e-06
ANY = pl.BlockSpec(memory_space=pl.ANY)
SMEM = pl.BlockSpec(memory_space=pltpu.SMEM)
VMEM = pl.BlockSpec(memory_space=pltpu.VMEM)
PARAMS = pltpu.CompilerParams(vmem_limit_bytes=16 * 1024 * 1024)
CONTRACT_LAST = (((1,), (1,)), ((), ()))


class Sizes:
    def __init__(self, queries, block_perm):
        self.ctx = lax.axis_size("ctx")
        self.heads = block_perm.shape[0]
        self.blocks = block_perm.shape[1] // self.ctx
        self.tokens, self.width = queries.shape
        self.block_len = self.tokens // self.blocks
        self.head_dim = self.width // self.heads
        self.capacity = self.heads // 2
        self.full = self.ctx * self.capacity == self.heads * self.blocks
        self.exponent = math.log2(math.e) / math.sqrt(self.head_dim)

    def tile(self, block, head):
        rows = pl.ds(pl.multiple_of(block * self.block_len, self.block_len), self.block_len)
        return rows, pl.ds(pl.multiple_of(head * self.head_dim, self.head_dim), self.head_dim)

    def send_shape(self):
        return (2, self.capacity, self.block_len, self.head_dim)


def schedule(ctx):
    if ctx == 8:
        steps = [("base", [2]), ("prev", [5]), ((0, 1), [3])]
        return [6, 7, 4, 1], steps + [((d,), []) for d in (6, 7, 4, 2)] + [((5, 3), [])]
    rest = list(range(1, ctx))
    return rest, [("base", []), ("prev", []), ((0,), [])] + [((d,), []) for d in rest]


def near(array):
    return pltpu.with_memory_space_constraint(array, pltpu.VMEM)


def far(array):
    return pltpu.with_memory_space_constraint(array, pltpu.HBM)


def wanted(sizes, d, rank, perm):
    start = jnp.bitwise_xor(rank, d) * sizes.blocks
    slot = jnp.int32(0)
    for head in range(sizes.heads):
        found = jnp.int32(-1)
        for j in range(sizes.blocks):
            source = perm[head, start + j] - rank * sizes.blocks
            found = jnp.where((source >= 0) & (source < sizes.blocks), source, found)
        yield head, found, slot
        slot = slot + (found >= 0).astype(jnp.int32)


def pack_near(sizes, items, which, array, send):
    for head, found, slot in items:

        @pl.when(found >= 0)
        def _():
            send[which, slot] = array[sizes.tile(found, head)]


def pack_both(sizes, d, rank, perm, keys, values, send):
    items = list(wanted(sizes, d, rank, perm))
    for which, array in enumerate((keys, values)):
        pack_near(sizes, items, which, array, send)


def first_kernel(
    sizes, partners, rank_ref, perm_far, keys, values, near_keys, near_values, last, *rest
):
    sends, (perm, perm_sem, sems) = rest[:-3], rest[-3:]
    perm_copy = pltpu.make_async_copy(perm_far, perm, perm_sem.at[0])
    perm_copy.start()
    copies = [
        pltpu.make_async_copy(keys, near_keys, sems.at[0]),
        pltpu.make_async_copy(values, near_values, sems.at[1]),
    ]
    for copy in copies:
        copy.start()
    perm_copy.wait()
    found = [list(wanted(sizes, d, rank_ref[0], perm)) for d in partners]
    for i, (copy, array) in enumerate(zip(copies, (near_keys, near_values))):
        copy.wait()
        last[i] = array[sizes.tokens - sizes.block_len :]
        for items, send in zip(found, sends):
            pack_near(sizes, items, i, array, send)


def first_sends(sizes, partners, rank, perm, keys, values):
    near_keys, near_values, last, *sends = pl.pallas_call(
        functools.partial(first_kernel, sizes, partners),
        out_shape=[pltpu.VMEM(keys.shape, keys.dtype)] * 2
        + [pltpu.VMEM((2, sizes.block_len, sizes.width), keys.dtype)]
        + [pltpu.VMEM(sizes.send_shape(), keys.dtype)] * len(partners),
        in_specs=[SMEM, ANY, ANY, ANY],
        out_specs=[VMEM] * (3 + len(partners)),
        scratch_shapes=[
            pltpu.SMEM(perm.shape, perm.dtype),
            pltpu.SemaphoreType.DMA((1,)),
            pltpu.SemaphoreType.DMA((2,)),
        ],
        compiler_params=PARAMS,
        cost_estimate=pl.CostEstimate(flops=1, bytes_accessed=1, transcendentals=0),
        name="first_sends",
    )(rank, far(perm), far(keys), far(values))
    return near_keys, near_values, last, dict(zip(partners, sends))


def weigh(sizes, scores, peak, values):
    weights = jnp.exp2((scores - peak) * sizes.exponent).astype(jnp.bfloat16)
    ones = jnp.ones(values.shape, values.dtype)
    both = jnp.concatenate([values, ones], axis=1)
    return jnp.dot(weights, both, preferred_element_type=jnp.float32)


def list_matches(sizes, rank, perm, table, counts):
    for d in range(sizes.ctx):
        counts[d] = 0
        if not sizes.full:
            for c in range(sizes.capacity):
                table[d * sizes.capacity + c] = -1
    for head in range(sizes.heads):
        for j in range(sizes.blocks):
            source = perm[head, rank * sizes.blocks + j]
            d = jnp.bitwise_xor(lax.div(source, sizes.blocks), rank)
            slot = counts[d]
            counts[d] = slot + 1
            table[d * sizes.capacity + slot] = (head * sizes.blocks + j) * sizes.blocks + lax.rem(
                source, sizes.blocks
            )


def base_kernel(sizes, partners, rank_ref, perm, queries, keys, values, *rest):
    near_queries, mixture, weight_sum, peaks, squares, table, *sends = rest[: 6 + len(partners)]
    counts, sem = rest[6 + len(partners) :]
    copy = pltpu.make_async_copy(queries, near_queries, sem.at[0])
    copy.start()
    rank = rank_ref[0]
    for d, send in zip(partners, sends):
        pack_both(sizes, d, rank, perm, keys, values, send)
    list_matches(sizes, rank, perm, table, counts)
    squares[...] = jnp.zeros_like(squares)
    copy.wait()
    n = sizes.block_len

    def one_head(head, _):
        columns = sizes.tile(0, head)[1]
        for j in range(sizes.blocks):
            here = slice(j * n, (j + 1) * n), columns
            context = slice(max(j - 1, 0) * n, (j + 1) * n), columns
            scores = lax.dot_general(
                near_queries[here],
                keys[context],
                CONTRACT_LAST,
                preferred_element_type=jnp.float32,
            )
            row = lax.broadcasted_iota(jnp.int32, (n, n), 0)
            column = lax.broadcasted_iota(jnp.int32, (n, n), 1)
            own = jnp.where(row >= column, scores[:, -n:], -jnp.inf)
            scores = own if j == 0 else jnp.concatenate([scores[:, :n], own], axis=1)
            peak = jnp.max(scores, axis=1, keepdims=True)
            total = weigh(sizes, scores, peak, values[context])
            mixture[here] = total[:, : sizes.head_dim]
            weight_sum[here] = total[:, sizes.head_dim :]
            peaks[here] = jnp.broadcast_to(peak, (n, sizes.head_dim))
        return 0

    lax.fori_loop(0, sizes.heads, one_head, 0)


def base(sizes, partners, rank, perm, queries, keys, values):
    state = pltpu.VMEM((sizes.tokens, sizes.width), jnp.float32)
    count = sizes.heads * sizes.blocks
    near_queries, *rest = pl.pallas_call(
        functools.partial(base_kernel, sizes, partners),
        out_shape=[
            pltpu.VMEM(queries.shape, queries.dtype),
            state,
            state,
            state,
            pltpu.VMEM((sizes.tokens, sizes.head_dim), jnp.float32),
            jax.ShapeDtypeStruct((sizes.ctx * sizes.capacity,), jnp.int32),
        ]
        + [pltpu.VMEM(sizes.send_shape(), keys.dtype)] * len(partners),
        in_specs=[SMEM, SMEM, ANY, VMEM, VMEM],
        out_specs=[VMEM] * 5 + [SMEM] + [VMEM] * len(partners),
        scratch_shapes=[
            pltpu.SMEM((sizes.ctx,), jnp.int32),
            pltpu.SemaphoreType.DMA((1,)),
        ],
        compiler_params=PARAMS,
        cost_estimate=pl.CostEstimate(flops=1, bytes_accessed=1, transcendentals=0),
        name="base_items",
    )(rank, perm, far(queries), near(keys), near(values))
    return near_queries, tuple(rest[:4]), rest[4], dict(zip(partners, rest[5:]))


def update_kernel(sizes, group, partners, last, rank_ref, perm, table, queries, keys, values, *rest):
    before = group == "prev"
    remote = ["prev"] if before else [d for d in group if d > 0]
    received, rest = dict(zip(remote, rest)), rest[len(remote) + 4 :]
    mixture, weight_sum, peaks, squares = rest[:4]
    rank = rank_ref[0]
    for d, send in zip(partners, rest[4:]):
        pack_both(sizes, d, rank, perm, keys, values, send)

    def add(here, key_tile, value_tile):
        scores = lax.dot_general(
            queries[here], key_tile, CONTRACT_LAST, preferred_element_type=jnp.float32
        )
        old = peaks[here]
        new = jnp.maximum(old, jnp.max(scores, axis=1, keepdims=True))
        wide = jnp.concatenate([new] * (sizes.block_len // sizes.head_dim), axis=1)
        total = weigh(sizes, scores, wide, value_tile)
        shrink = jnp.exp2((old - new) * sizes.exponent)
        mixed = mixture[here] * shrink + total[:, : sizes.head_dim]
        summed = weight_sum[here] * shrink + total[:, sizes.head_dim :]
        if before:
            mixture[here] = mixed
            weight_sum[here] = summed
            peaks[here] = new
        else:
            attended = mixed / summed
            mixture[here] = attended
            squares[here[0]] += attended * attended

    if before:

        @pl.when(rank > 0)
        def _():
            for head in range(sizes.heads):
                here = sizes.tile(0, head)
                add(here, *[received["prev"][i, :, here[1]] for i in range(2)])

        return

    def match(d, c, item):
        head = lax.div(item, sizes.blocks * sizes.blocks)
        here = sizes.tile(lax.rem(lax.div(item, sizes.blocks), sizes.blocks), head)
        if d > 0:
            add(here, received[d][0, c], received[d][1, c])
        else:
            there = sizes.tile(lax.rem(item, sizes.blocks), head)
            add(here, keys[there], values[there])

    for d in group:
        for c in range(sizes.capacity):
            item = table[d * sizes.capacity + c]
            if sizes.full:
                match(d, c, item)
            else:
                pl.when(item >= 0)(functools.partial(match, d, c, item))
    if last:
        rest[4][...] = lax.dot_general(
            jnp.ones((8, sizes.head_dim), jnp.float32),
            squares[...],
            CONTRACT_LAST,
            precision=lax.Precision.HIGHEST,
            preferred_element_type=jnp.float32,
        )[:1]


def update(sizes, group, partners, last, rank, perm, table, queries, keys, values, received, state):
    remote = [received["prev"]] if group == "prev" else [received[d] for d in group if d > 0]
    arrays = [near(a) for a in [queries, keys, values] + remote + list(state)]
    count = sizes.heads if group == "prev" else len(group) * sizes.capacity
    out_shape = [pltpu.VMEM(a.shape, a.dtype) for a in state]
    out_shape += [pltpu.VMEM(sizes.send_shape(), keys.dtype)] * len(partners)
    if last:
        out_shape.append(jax.ShapeDtypeStruct((1, sizes.tokens), jnp.float32))
    first_state = 3 + len(arrays) - len(state)
    out = pl.pallas_call(
        functools.partial(update_kernel, sizes, group, partners, last),
        out_shape=out_shape,
        in_specs=[SMEM] * 3 + [VMEM] * len(arrays),
        out_specs=[VMEM] * len(out_shape),
        input_output_aliases={first_state + i: i for i in range(len(state))},
        compiler_params=PARAMS,
        cost_estimate=pl.CostEstimate(flops=1, bytes_accessed=1, transcendentals=0),
        name="update_items",
    )(rank, perm, table, *arrays)
    return tuple(out[:4]), out[4:]


def scale_kernel(width, block_len, gain, *rest):
    sums, (attended, out, buffer, sems) = rest[:-4], rest[-4:]
    total = sums[0][...]
    for other in sums[1:]:
        total = total + other[...]
    inverse = lax.rsqrt(total / width + NORM_EPS)
    steps = attended.shape[0] // block_len
    copies = []
    for i in range(steps):
        rows = slice(i * block_len, (i + 1) * block_len)
        column = jnp.transpose(jnp.broadcast_to(inverse[:, rows], (8, block_len)))[:, :1]
        buffer[rows] = (attended[rows] * column * gain[...]).astype(out.dtype)
        copies.append(pltpu.make_async_copy(buffer.at[rows], out.at[rows], sems.at[i]))
        copies[i].start()
    for copy in copies:
        copy.wait()


def scaled(attended, sums, gain, width, block_len):
    tok_rows, row_width = attended.shape
    return pl.pallas_call(
        functools.partial(scale_kernel, width, block_len),
        out_shape=jax.ShapeDtypeStruct((tok_rows, row_width), jnp.bfloat16),
        in_specs=[VMEM] * (len(sums) + 2),
        out_specs=ANY,
        scratch_shapes=[
            pltpu.VMEM((tok_rows, row_width), jnp.bfloat16),
            pltpu.SemaphoreType.DMA((tok_rows // block_len,)),
        ],
        compiler_params=PARAMS,
        name="scale_rows",
    )(gain.reshape(1, row_width), *sums, near(attended))


def per_device(queries, keys, values, block_perm, norm_gain):
    sizes = Sizes(queries, block_perm)
    head_size = lax.axis_size("head")
    rank = lax.axis_index("ctx").astype(jnp.int32).reshape(1)
    received = {}

    def exchange(sends):
        for d, array in sends.items():
            with jax.named_scope(f"match{d}"):
                route = [(i, i ^ d) for i in range(sizes.ctx)]
                received[d] = lax.ppermute(array, "ctx", route)

    first, steps = schedule(sizes.ctx)
    keys, values, last_block, sends = first_sends(sizes, first, rank, block_perm, keys, values)
    with jax.named_scope("previous"):
        route = [(i, i + 1) for i in range(sizes.ctx - 1)]
        received["prev"] = lax.ppermute(last_block, "ctx", route)
    exchange(sends)
    queries, state, table, sends = base(
        sizes, steps[0][1], rank, block_perm, queries, keys, values
    )
    exchange(sends)
    for group, partners in steps[1:]:
        last = group == steps[-1][0]
        state, extra = update(
            sizes, group, partners, last, rank, block_perm, table, queries, keys, values,
            received, state,
        )
        exchange(dict(zip(partners, extra)))
    sums = [extra[-1]]
    for d in range(1, head_size):
        sums.append(lax.ppermute(sums[0], "head", [(i, i ^ d) for i in range(head_size)]))
    return scaled(state[0], sums, norm_gain, sizes.width * head_size, sizes.block_len)


def solution(mesh):
    placed = (P("ctx", "head"), P("ctx", "head"), P("ctx", "head"), P("head", None), P("head"))
    return jax.shard_map(
        per_device, mesh=mesh, in_specs=placed, out_specs=P("ctx", "head"), check_vma=False
    )
```

```python
import functools
import math

import jax
import jax.numpy as jnp
from jax import lax
from jax.experimental import pallas as pl
from jax.experimental.pallas import tpu as pltpu
from jax.sharding import PartitionSpec as P

NORM_EPS = 1e-06
ANY = pl.BlockSpec(memory_space=pl.ANY)
SMEM = pl.BlockSpec(memory_space=pltpu.SMEM)
VMEM = pl.BlockSpec(memory_space=pltpu.VMEM)
PARAMS = pltpu.CompilerParams(vmem_limit_bytes=16 * 1024 * 1024)
CONTRACT_LAST = (((1,), (1,)), ((), ()))


class Sizes:
    def __init__(self, queries, block_perm):
        self.ctx = lax.axis_size("ctx")
        self.heads = block_perm.shape[0]
        self.blocks = block_perm.shape[1] // self.ctx
        self.tokens, self.width = queries.shape
        self.block_len = self.tokens // self.blocks
        self.head_dim = self.width // self.heads
        self.capacity = self.heads // 2
        self.full = self.ctx * self.capacity == self.heads * self.blocks
        self.exponent = math.log2(math.e) / math.sqrt(self.head_dim)

    def tile(self, block, head):
        rows = pl.ds(pl.multiple_of(block * self.block_len, self.block_len), self.block_len)
        return rows, pl.ds(pl.multiple_of(head * self.head_dim, self.head_dim), self.head_dim)

    def send_shape(self):
        return (2, self.capacity, self.block_len, self.head_dim)


def schedule(ctx):
    if ctx == 8:
        steps = [("base", [2]), ("prev", [5]), ((0, 1), [3])]
        return [6, 7, 4, 1], steps + [((d,), []) for d in (6, 7, 4, 2)] + [((5, 3), [])]
    rest = list(range(1, ctx))
    return rest, [("base", []), ("prev", []), ((0,), [])] + [((d,), []) for d in rest]


def near(array):
    return pltpu.with_memory_space_constraint(array, pltpu.VMEM)


def far(array):
    return pltpu.with_memory_space_constraint(array, pltpu.HBM)


def wanted(sizes, d, rank, perm):
    start = jnp.bitwise_xor(rank, d) * sizes.blocks
    slot = jnp.int32(0)
    for head in range(sizes.heads):
        found = jnp.int32(-1)
        for j in range(sizes.blocks):
            source = perm[head, start + j] - rank * sizes.blocks
            found = jnp.where((source >= 0) & (source < sizes.blocks), source, found)
        yield head, found, slot
        slot = slot + (found >= 0).astype(jnp.int32)


def pack_near(sizes, items, which, array, send):
    for head, found, slot in items:

        @pl.when(found >= 0)
        def _():
            send[which, slot] = array[sizes.tile(found, head)]


def pack_both(sizes, d, rank, perm, keys, values, send):
    items = list(wanted(sizes, d, rank, perm))
    for which, array in enumerate((keys, values)):
        pack_near(sizes, items, which, array, send)


def last_kernel(block_len, keys, values, last, sems):
    rows = pl.ds(keys.shape[0] - block_len, block_len)
    copies = [
        pltpu.make_async_copy(array.at[rows], last.at[i], sems.at[i])
        for i, array in enumerate((keys, values))
    ]
    for copy in copies:
        copy.start()
    for copy in copies:
        copy.wait()


def last_blocks(sizes, keys, values):
    return pl.pallas_call(
        functools.partial(last_kernel, sizes.block_len),
        out_shape=pltpu.VMEM((2, sizes.block_len, sizes.width), keys.dtype),
        in_specs=[ANY, ANY],
        out_specs=VMEM,
        scratch_shapes=[pltpu.SemaphoreType.DMA((2,))],
        compiler_params=PARAMS,
        cost_estimate=pl.CostEstimate(flops=1, bytes_accessed=1, transcendentals=0),
        name="last_blocks",
    )(far(keys), far(values))


def first_kernel(
    sizes, partners, rank_ref, perm_far, keys, values, near_keys, near_values, *rest
):
    sends, (perm, perm_sem, sems) = rest[:-3], rest[-3:]
    perm_copy = pltpu.make_async_copy(perm_far, perm, perm_sem.at[0])
    perm_copy.start()
    copies = [
        pltpu.make_async_copy(keys, near_keys, sems.at[0]),
        pltpu.make_async_copy(values, near_values, sems.at[1]),
    ]
    for copy in copies:
        copy.start()
    perm_copy.wait()
    found = [list(wanted(sizes, d, rank_ref[0], perm)) for d in partners]
    for i, (copy, array) in enumerate(zip(copies, (near_keys, near_values))):
        copy.wait()
        for items, send in zip(found, sends):
            pack_near(sizes, items, i, array, send)


def first_sends(sizes, partners, rank, perm, keys, values):
    near_keys, near_values, *sends = pl.pallas_call(
        functools.partial(first_kernel, sizes, partners),
        out_shape=[pltpu.VMEM(keys.shape, keys.dtype)] * 2
        + [pltpu.VMEM(sizes.send_shape(), keys.dtype)] * len(partners),
        in_specs=[SMEM, ANY, ANY, ANY],
        out_specs=[VMEM] * (2 + len(partners)),
        scratch_shapes=[
            pltpu.SMEM(perm.shape, perm.dtype),
            pltpu.SemaphoreType.DMA((1,)),
            pltpu.SemaphoreType.DMA((2,)),
        ],
        compiler_params=PARAMS,
        cost_estimate=pl.CostEstimate(flops=1, bytes_accessed=1, transcendentals=0),
        name="first_sends",
    )(rank, far(perm), far(keys), far(values))
    return near_keys, near_values, dict(zip(partners, sends))


def weigh(sizes, scores, peak, values):
    weights = jnp.exp2((scores - peak) * sizes.exponent).astype(jnp.bfloat16)
    ones = jnp.ones(values.shape, values.dtype)
    both = jnp.concatenate([values, ones], axis=1)
    return jnp.dot(weights, both, preferred_element_type=jnp.float32)


def list_matches(sizes, rank, perm, table, counts):
    for d in range(sizes.ctx):
        counts[d] = 0
        if not sizes.full:
            for c in range(sizes.capacity):
                table[d * sizes.capacity + c] = -1
    for head in range(sizes.heads):
        for j in range(sizes.blocks):
            source = perm[head, rank * sizes.blocks + j]
            d = jnp.bitwise_xor(lax.div(source, sizes.blocks), rank)
            slot = counts[d]
            counts[d] = slot + 1
            table[d * sizes.capacity + slot] = (head * sizes.blocks + j) * sizes.blocks + lax.rem(
                source, sizes.blocks
            )


def base_kernel(sizes, partners, rank_ref, perm, queries, keys, values, *rest):
    near_queries, mixture, weight_sum, peaks, squares, table, *sends = rest[: 6 + len(partners)]
    counts, sem = rest[6 + len(partners) :]
    copy = pltpu.make_async_copy(queries, near_queries, sem.at[0])
    copy.start()
    rank = rank_ref[0]
    for d, send in zip(partners, sends):
        pack_both(sizes, d, rank, perm, keys, values, send)
    list_matches(sizes, rank, perm, table, counts)
    squares[...] = jnp.zeros_like(squares)
    copy.wait()
    n = sizes.block_len

    def one_head(head, _):
        columns = sizes.tile(0, head)[1]
        for j in range(sizes.blocks):
            here = slice(j * n, (j + 1) * n), columns
            context = slice(max(j - 1, 0) * n, (j + 1) * n), columns
            scores = lax.dot_general(
                near_queries[here],
                keys[context],
                CONTRACT_LAST,
                preferred_element_type=jnp.float32,
            )
            row = lax.broadcasted_iota(jnp.int32, (n, n), 0)
            column = lax.broadcasted_iota(jnp.int32, (n, n), 1)
            own = jnp.where(row >= column, scores[:, -n:], -jnp.inf)
            scores = own if j == 0 else jnp.concatenate([scores[:, :n], own], axis=1)
            peak = jnp.max(scores, axis=1, keepdims=True)
            total = weigh(sizes, scores, peak, values[context])
            mixture[here] = total[:, : sizes.head_dim]
            weight_sum[here] = total[:, sizes.head_dim :]
            peaks[here] = jnp.broadcast_to(peak, (n, sizes.head_dim))
        return 0

    lax.fori_loop(0, sizes.heads, one_head, 0)


def base(sizes, partners, rank, perm, queries, keys, values):
    state = pltpu.VMEM((sizes.tokens, sizes.width), jnp.float32)
    count = sizes.heads * sizes.blocks
    near_queries, *rest = pl.pallas_call(
        functools.partial(base_kernel, sizes, partners),
        out_shape=[
            pltpu.VMEM(queries.shape, queries.dtype),
            state,
            state,
            state,
            pltpu.VMEM((sizes.tokens, sizes.head_dim), jnp.float32),
            jax.ShapeDtypeStruct((sizes.ctx * sizes.capacity,), jnp.int32),
        ]
        + [pltpu.VMEM(sizes.send_shape(), keys.dtype)] * len(partners),
        in_specs=[SMEM, SMEM, ANY, VMEM, VMEM],
        out_specs=[VMEM] * 5 + [SMEM] + [VMEM] * len(partners),
        scratch_shapes=[
            pltpu.SMEM((sizes.ctx,), jnp.int32),
            pltpu.SemaphoreType.DMA((1,)),
        ],
        compiler_params=PARAMS,
        cost_estimate=pl.CostEstimate(flops=1, bytes_accessed=1, transcendentals=0),
        name="base_items",
    )(rank, perm, far(queries), near(keys), near(values))
    return near_queries, tuple(rest[:4]), rest[4], dict(zip(partners, rest[5:]))


def update_kernel(sizes, group, partners, last, rank_ref, perm, table, queries, keys, values, *rest):
    before = group == "prev"
    remote = ["prev"] if before else [d for d in group if d > 0]
    received, rest = dict(zip(remote, rest)), rest[len(remote) + 4 :]
    mixture, weight_sum, peaks, squares = rest[:4]
    rank = rank_ref[0]
    for d, send in zip(partners, rest[4:]):
        pack_both(sizes, d, rank, perm, keys, values, send)

    def add(here, key_tile, value_tile):
        scores = lax.dot_general(
            queries[here], key_tile, CONTRACT_LAST, preferred_element_type=jnp.float32
        )
        old = peaks[here]
        new = jnp.maximum(old, jnp.max(scores, axis=1, keepdims=True))
        wide = jnp.concatenate([new] * (sizes.block_len // sizes.head_dim), axis=1)
        total = weigh(sizes, scores, wide, value_tile)
        shrink = jnp.exp2((old - new) * sizes.exponent)
        mixed = mixture[here] * shrink + total[:, : sizes.head_dim]
        summed = weight_sum[here] * shrink + total[:, sizes.head_dim :]
        if before:
            mixture[here] = mixed
            weight_sum[here] = summed
            peaks[here] = new
        else:
            attended = mixed / summed
            mixture[here] = attended
            squares[here[0]] += attended * attended

    if before:

        @pl.when(rank > 0)
        def _():
            for head in range(sizes.heads):
                here = sizes.tile(0, head)
                add(here, *[received["prev"][i, :, here[1]] for i in range(2)])

        return

    def match(d, c, item):
        head = lax.div(item, sizes.blocks * sizes.blocks)
        here = sizes.tile(lax.rem(lax.div(item, sizes.blocks), sizes.blocks), head)
        if d > 0:
            add(here, received[d][0, c], received[d][1, c])
        else:
            there = sizes.tile(lax.rem(item, sizes.blocks), head)
            add(here, keys[there], values[there])

    for d in group:
        for c in range(sizes.capacity):
            item = table[d * sizes.capacity + c]
            if sizes.full:
                match(d, c, item)
            else:
                pl.when(item >= 0)(functools.partial(match, d, c, item))
    if last:
        rest[4][...] = lax.dot_general(
            jnp.ones((8, sizes.head_dim), jnp.float32),
            squares[...],
            CONTRACT_LAST,
            precision=lax.Precision.HIGHEST,
            preferred_element_type=jnp.float32,
        )[:1]


def update(sizes, group, partners, last, rank, perm, table, queries, keys, values, received, state):
    remote = [received["prev"]] if group == "prev" else [received[d] for d in group if d > 0]
    arrays = [near(a) for a in [queries, keys, values] + remote + list(state)]
    count = sizes.heads if group == "prev" else len(group) * sizes.capacity
    out_shape = [pltpu.VMEM(a.shape, a.dtype) for a in state]
    out_shape += [pltpu.VMEM(sizes.send_shape(), keys.dtype)] * len(partners)
    if last:
        out_shape.append(jax.ShapeDtypeStruct((1, sizes.tokens), jnp.float32))
    first_state = 3 + len(arrays) - len(state)
    out = pl.pallas_call(
        functools.partial(update_kernel, sizes, group, partners, last),
        out_shape=out_shape,
        in_specs=[SMEM] * 3 + [VMEM] * len(arrays),
        out_specs=[VMEM] * len(out_shape),
        input_output_aliases={first_state + i: i for i in range(len(state))},
        compiler_params=PARAMS,
        cost_estimate=pl.CostEstimate(flops=1, bytes_accessed=1, transcendentals=0),
        name="update_items",
    )(rank, perm, table, *arrays)
    return tuple(out[:4]), out[4:]


def scale_kernel(width, block_len, gain, *rest):
    sums, (attended, out, buffer, sems) = rest[:-4], rest[-4:]
    total = sums[0][...]
    for other in sums[1:]:
        total = total + other[...]
    inverse = lax.rsqrt(total / width + NORM_EPS)
    steps = attended.shape[0] // block_len
    copies = []
    for i in range(steps):
        rows = slice(i * block_len, (i + 1) * block_len)
        column = jnp.transpose(jnp.broadcast_to(inverse[:, rows], (8, block_len)))[:, :1]
        buffer[rows] = (attended[rows] * column * gain[...]).astype(out.dtype)
        copies.append(pltpu.make_async_copy(buffer.at[rows], out.at[rows], sems.at[i]))
        copies[i].start()
    for copy in copies:
        copy.wait()


def scaled(attended, sums, gain, width, block_len):
    tok_rows, row_width = attended.shape
    return pl.pallas_call(
        functools.partial(scale_kernel, width, block_len),
        out_shape=jax.ShapeDtypeStruct((tok_rows, row_width), jnp.bfloat16),
        in_specs=[VMEM] * (len(sums) + 2),
        out_specs=ANY,
        scratch_shapes=[
            pltpu.VMEM((tok_rows, row_width), jnp.bfloat16),
            pltpu.SemaphoreType.DMA((tok_rows // block_len,)),
        ],
        compiler_params=PARAMS,
        name="scale_rows",
    )(gain.reshape(1, row_width), *sums, near(attended))


def per_device(queries, keys, values, block_perm, norm_gain):
    sizes = Sizes(queries, block_perm)
    head_size = lax.axis_size("head")
    rank = lax.axis_index("ctx").astype(jnp.int32).reshape(1)
    received = {}

    def exchange(sends):
        for d, array in sends.items():
            with jax.named_scope(f"match{d}"):
                route = [(i, i ^ d) for i in range(sizes.ctx)]
                received[d] = lax.ppermute(array, "ctx", route)

    first, steps = schedule(sizes.ctx)
    last_block = last_blocks(sizes, keys, values)
    keys, values, sends = first_sends(sizes, first, rank, block_perm, keys, values)
    with jax.named_scope("previous"):
        route = [(i, i + 1) for i in range(sizes.ctx - 1)]
        received["prev"] = lax.ppermute(last_block, "ctx", route)
    exchange(sends)
    queries, state, table, sends = base(
        sizes, steps[0][1], rank, block_perm, queries, keys, values
    )
    exchange(sends)
    for group, partners in steps[1:]:
        last = group == steps[-1][0]
        state, extra = update(
            sizes, group, partners, last, rank, block_perm, table, queries, keys, values,
            received, state,
        )
        exchange(dict(zip(partners, extra)))
    sums = [extra[-1]]
    for d in range(1, head_size):
        sums.append(lax.ppermute(sums[0], "head", [(i, i ^ d) for i in range(head_size)]))
    return scaled(state[0], sums, norm_gain, sizes.width * head_size, sizes.block_len)


def solution(mesh):
    placed = (P("ctx", "head"), P("ctx", "head"), P("ctx", "head"), P("head", None), P("head"))
    return jax.shard_map(
        per_device, mesh=mesh, in_specs=placed, out_specs=P("ctx", "head"), check_vma=False
    )
```

```python
import functools
import math

import jax
import jax.numpy as jnp
from jax import lax
from jax.experimental import pallas as pl
from jax.experimental.pallas import tpu as pltpu
from jax.sharding import PartitionSpec as P

NORM_EPS = 1e-06
ANY = pl.BlockSpec(memory_space=pl.ANY)
SMEM = pl.BlockSpec(memory_space=pltpu.SMEM)
VMEM = pl.BlockSpec(memory_space=pltpu.VMEM)
PARAMS = pltpu.CompilerParams(vmem_limit_bytes=16 * 1024 * 1024)
CONTRACT_LAST = (((1,), (1,)), ((), ()))


class Sizes:
    def __init__(self, queries, block_perm):
        self.ctx = lax.axis_size("ctx")
        self.heads = block_perm.shape[0]
        self.blocks = block_perm.shape[1] // self.ctx
        self.tokens, self.width = queries.shape
        self.block_len = self.tokens // self.blocks
        self.head_dim = self.width // self.heads
        self.capacity = self.heads // 2
        self.full = self.ctx * self.capacity == self.heads * self.blocks
        self.exponent = math.log2(math.e) / math.sqrt(self.head_dim)

    def tile(self, block, head):
        rows = pl.ds(pl.multiple_of(block * self.block_len, self.block_len), self.block_len)
        return rows, pl.ds(pl.multiple_of(head * self.head_dim, self.head_dim), self.head_dim)

    def send_shape(self, message):
        _, low, high = message
        return (2, high - low, self.block_len, self.head_dim)


def schedule(ctx, capacity):
    whole = {d: (d, 0, capacity) for d in range(ctx)}
    if ctx == 8:
        half = capacity // 2
        (five, last_five), (three, last_three) = [
            ((d, 0, half), (d, half, capacity)) for d in (5, 3)
        ]
        steps = [
            ("base", [whole[2]]),
            ("prev", [five]),
            ((whole[0], whole[1]), [three]),
            ((whole[6],), [last_five]),
            ((whole[7],), [last_three]),
            ((whole[4],), []),
            ((whole[2],), []),
            ((five,), []),
            ((three,), []),
            ((last_five, last_three), []),
        ]
        return [whole[d] for d in (6, 7, 4, 1)], steps
    rest = [whole[d] for d in range(1, ctx)]
    return rest, [("base", []), ("prev", []), ((whole[0],), [])] + [((m,), []) for m in rest]


def near(array):
    return pltpu.with_memory_space_constraint(array, pltpu.VMEM)


def far(array):
    return pltpu.with_memory_space_constraint(array, pltpu.HBM)


def wanted(sizes, d, rank, perm):
    start = jnp.bitwise_xor(rank, d) * sizes.blocks
    slot = jnp.int32(0)
    for head in range(sizes.heads):
        found = jnp.int32(-1)
        for j in range(sizes.blocks):
            source = perm[head, start + j] - rank * sizes.blocks
            found = jnp.where((source >= 0) & (source < sizes.blocks), source, found)
        yield head, found, slot
        slot = slot + (found >= 0).astype(jnp.int32)


def pack_near(sizes, message, items, which, array, send):
    _, low, high = message
    for head, found, slot in items:
        here = (found >= 0) & (slot >= low) & (slot < high)

        @pl.when(found >= 0 if high - low == sizes.capacity else here)
        def _():
            send[which, slot - low] = array[sizes.tile(found, head)]


def pack_both(sizes, message, rank, perm, keys, values, send):
    items = list(wanted(sizes, message[0], rank, perm))
    for which, array in enumerate((keys, values)):
        pack_near(sizes, message, items, which, array, send)


def last_kernel(block_len, keys, values, last, sems):
    rows = pl.ds(keys.shape[0] - block_len, block_len)
    copies = [
        pltpu.make_async_copy(array.at[rows], last.at[i], sems.at[i])
        for i, array in enumerate((keys, values))
    ]
    for copy in copies:
        copy.start()
    for copy in copies:
        copy.wait()


def last_blocks(sizes, keys, values):
    return pl.pallas_call(
        functools.partial(last_kernel, sizes.block_len),
        out_shape=pltpu.VMEM((2, sizes.block_len, sizes.width), keys.dtype),
        in_specs=[ANY, ANY],
        out_specs=VMEM,
        scratch_shapes=[pltpu.SemaphoreType.DMA((2,))],
        compiler_params=PARAMS,
        cost_estimate=pl.CostEstimate(flops=1, bytes_accessed=1, transcendentals=0),
        name="last_blocks",
    )(far(keys), far(values))


def first_kernel(
    sizes, partners, rank_ref, perm_far, keys, values, near_keys, near_values, *rest
):
    sends, (perm, perm_sem, sems) = rest[:-3], rest[-3:]
    perm_copy = pltpu.make_async_copy(perm_far, perm, perm_sem.at[0])
    perm_copy.start()
    copies = [
        pltpu.make_async_copy(keys, near_keys, sems.at[0]),
        pltpu.make_async_copy(values, near_values, sems.at[1]),
    ]
    for copy in copies:
        copy.start()
    perm_copy.wait()
    found = [list(wanted(sizes, m[0], rank_ref[0], perm)) for m in partners]
    for i, (copy, array) in enumerate(zip(copies, (near_keys, near_values))):
        copy.wait()
        for message, items, send in zip(partners, found, sends):
            pack_near(sizes, message, items, i, array, send)


def first_sends(sizes, partners, rank, perm, keys, values):
    near_keys, near_values, *sends = pl.pallas_call(
        functools.partial(first_kernel, sizes, partners),
        out_shape=[pltpu.VMEM(keys.shape, keys.dtype)] * 2
        + [pltpu.VMEM(sizes.send_shape(m), keys.dtype) for m in partners],
        in_specs=[SMEM, ANY, ANY, ANY],
        out_specs=[VMEM] * (2 + len(partners)),
        scratch_shapes=[
            pltpu.SMEM(perm.shape, perm.dtype),
            pltpu.SemaphoreType.DMA((1,)),
            pltpu.SemaphoreType.DMA((2,)),
        ],
        compiler_params=PARAMS,
        cost_estimate=pl.CostEstimate(flops=1, bytes_accessed=1, transcendentals=0),
        name="first_sends",
    )(rank, far(perm), far(keys), far(values))
    return near_keys, near_values, dict(zip(partners, sends))


def weigh(sizes, scores, peak, values):
    weights = jnp.exp2((scores - peak) * sizes.exponent).astype(jnp.bfloat16)
    ones = jnp.ones(values.shape, values.dtype)
    both = jnp.concatenate([values, ones], axis=1)
    return jnp.dot(weights, both, preferred_element_type=jnp.float32)


def list_matches(sizes, rank, perm, table, counts):
    for d in range(sizes.ctx):
        counts[d] = 0
        if not sizes.full:
            for c in range(sizes.capacity):
                table[d * sizes.capacity + c] = -1
    for head in range(sizes.heads):
        for j in range(sizes.blocks):
            source = perm[head, rank * sizes.blocks + j]
            d = jnp.bitwise_xor(lax.div(source, sizes.blocks), rank)
            slot = counts[d]
            counts[d] = slot + 1
            table[d * sizes.capacity + slot] = (head * sizes.blocks + j) * sizes.blocks + lax.rem(
                source, sizes.blocks
            )


def base_kernel(sizes, partners, rank_ref, perm, queries, keys, values, *rest):
    near_queries, mixture, weight_sum, peaks, squares, table, *sends = rest[: 6 + len(partners)]
    counts, sem = rest[6 + len(partners) :]
    copy = pltpu.make_async_copy(queries, near_queries, sem.at[0])
    copy.start()
    rank = rank_ref[0]
    for message, send in zip(partners, sends):
        pack_both(sizes, message, rank, perm, keys, values, send)
    list_matches(sizes, rank, perm, table, counts)
    squares[...] = jnp.zeros_like(squares)
    copy.wait()
    n = sizes.block_len

    def one_head(head, _):
        columns = sizes.tile(0, head)[1]
        for j in range(sizes.blocks):
            here = slice(j * n, (j + 1) * n), columns
            context = slice(max(j - 1, 0) * n, (j + 1) * n), columns
            scores = lax.dot_general(
                near_queries[here],
                keys[context],
                CONTRACT_LAST,
                preferred_element_type=jnp.float32,
            )
            row = lax.broadcasted_iota(jnp.int32, (n, n), 0)
            column = lax.broadcasted_iota(jnp.int32, (n, n), 1)
            own = jnp.where(row >= column, scores[:, -n:], -jnp.inf)
            scores = own if j == 0 else jnp.concatenate([scores[:, :n], own], axis=1)
            peak = jnp.max(scores, axis=1, keepdims=True)
            total = weigh(sizes, scores, peak, values[context])
            mixture[here] = total[:, : sizes.head_dim]
            weight_sum[here] = total[:, sizes.head_dim :]
            peaks[here] = jnp.broadcast_to(peak, (n, sizes.head_dim))
        return 0

    lax.fori_loop(0, sizes.heads, one_head, 0)


def base(sizes, partners, rank, perm, queries, keys, values):
    state = pltpu.VMEM((sizes.tokens, sizes.width), jnp.float32)
    count = sizes.heads * sizes.blocks
    near_queries, *rest = pl.pallas_call(
        functools.partial(base_kernel, sizes, partners),
        out_shape=[
            pltpu.VMEM(queries.shape, queries.dtype),
            state,
            state,
            state,
            pltpu.VMEM((sizes.tokens, sizes.head_dim), jnp.float32),
            jax.ShapeDtypeStruct((sizes.ctx * sizes.capacity,), jnp.int32),
        ]
        + [pltpu.VMEM(sizes.send_shape(m), keys.dtype) for m in partners],
        in_specs=[SMEM, SMEM, ANY, VMEM, VMEM],
        out_specs=[VMEM] * 5 + [SMEM] + [VMEM] * len(partners),
        scratch_shapes=[
            pltpu.SMEM((sizes.ctx,), jnp.int32),
            pltpu.SemaphoreType.DMA((1,)),
        ],
        compiler_params=PARAMS,
        cost_estimate=pl.CostEstimate(flops=1, bytes_accessed=1, transcendentals=0),
        name="base_items",
    )(rank, perm, far(queries), near(keys), near(values))
    return near_queries, tuple(rest[:4]), rest[4], dict(zip(partners, rest[5:]))


def update_kernel(sizes, group, partners, last, rank_ref, perm, table, queries, keys, values, *rest):
    before = group == "prev"
    remote = ["prev"] if before else [m for m in group if m[0] > 0]
    received, rest = dict(zip(remote, rest)), rest[len(remote) + 4 :]
    mixture, weight_sum, peaks, squares = rest[:4]
    rank = rank_ref[0]
    for message, send in zip(partners, rest[4:]):
        pack_both(sizes, message, rank, perm, keys, values, send)

    def add(here, key_tile, value_tile):
        scores = lax.dot_general(
            queries[here], key_tile, CONTRACT_LAST, preferred_element_type=jnp.float32
        )
        old = peaks[here]
        new = jnp.maximum(old, jnp.max(scores, axis=1, keepdims=True))
        wide = jnp.concatenate([new] * (sizes.block_len // sizes.head_dim), axis=1)
        total = weigh(sizes, scores, wide, value_tile)
        shrink = jnp.exp2((old - new) * sizes.exponent)
        mixed = mixture[here] * shrink + total[:, : sizes.head_dim]
        summed = weight_sum[here] * shrink + total[:, sizes.head_dim :]
        if before:
            mixture[here] = mixed
            weight_sum[here] = summed
            peaks[here] = new
        else:
            attended = mixed / summed
            mixture[here] = attended
            squares[here[0]] += attended * attended

    if before:

        @pl.when(rank > 0)
        def _():
            for head in range(sizes.heads):
                here = sizes.tile(0, head)
                add(here, *[received["prev"][i, :, here[1]] for i in range(2)])

        return

    def match(message, c, item):
        head = lax.div(item, sizes.blocks * sizes.blocks)
        here = sizes.tile(lax.rem(lax.div(item, sizes.blocks), sizes.blocks), head)
        if message[0] > 0:
            add(here, *[received[message][i, c - message[1]] for i in range(2)])
        else:
            there = sizes.tile(lax.rem(item, sizes.blocks), head)
            add(here, keys[there], values[there])

    for message in group:
        d, low, high = message
        for c in range(low, high):
            item = table[d * sizes.capacity + c]
            if sizes.full:
                match(message, c, item)
            else:
                pl.when(item >= 0)(functools.partial(match, message, c, item))
    if last:
        ones = jnp.ones((8, sizes.head_dim), jnp.bfloat16)
        rest_of = squares[...]
        total = None
        for _ in range(3):
            part = rest_of.astype(jnp.bfloat16)
            rest_of = rest_of - part.astype(jnp.float32)
            summed = lax.dot_general(ones, part, CONTRACT_LAST, preferred_element_type=jnp.float32)
            total = summed if total is None else total + summed
        rest[4][...] = total[:1]


def update(sizes, group, partners, last, rank, perm, table, queries, keys, values, received, state):
    remote = ["prev"] if group == "prev" else [m for m in group if m[0] > 0]
    remote = [received[m] for m in remote]
    arrays = [near(a) for a in [queries, keys, values] + remote + list(state)]
    out_shape = [pltpu.VMEM(a.shape, a.dtype) for a in state]
    out_shape += [pltpu.VMEM(sizes.send_shape(m), keys.dtype) for m in partners]
    if last:
        out_shape.append(jax.ShapeDtypeStruct((1, sizes.tokens), jnp.float32))
    first_state = 3 + len(arrays) - len(state)
    out = pl.pallas_call(
        functools.partial(update_kernel, sizes, group, partners, last),
        out_shape=out_shape,
        in_specs=[SMEM] * 3 + [VMEM] * len(arrays),
        out_specs=[VMEM] * len(out_shape),
        input_output_aliases={first_state + i: i for i in range(len(state))},
        compiler_params=PARAMS,
        cost_estimate=pl.CostEstimate(flops=1, bytes_accessed=1, transcendentals=0),
        name="update_items",
    )(rank, perm, table, *arrays)
    return tuple(out[:4]), out[4:]


def scale_kernel(width, step, gain, *rest):
    sums, (attended, out, buffer, sems) = rest[:-4], rest[-4:]
    total = sums[0][...]
    for other in sums[1:]:
        total = total + other[...]
    inverse = lax.rsqrt(total / width + NORM_EPS)
    steps = attended.shape[0] // step
    copies = []
    for i in range(steps):
        rows = slice(i * step, (i + 1) * step)
        column = jnp.transpose(jnp.broadcast_to(inverse[:, rows], (8, step)))[:, :1]
        buffer[rows] = (attended[rows] * column * gain[...]).astype(out.dtype)
        copies.append(pltpu.make_async_copy(buffer.at[rows], out.at[rows], sems.at[i]))
        copies[i].start()
    for copy in copies:
        copy.wait()


def scaled(attended, sums, gain, width, step):
    tok_rows, row_width = attended.shape
    return pl.pallas_call(
        functools.partial(scale_kernel, width, step),
        out_shape=jax.ShapeDtypeStruct((tok_rows, row_width), jnp.bfloat16),
        in_specs=[VMEM] * (len(sums) + 2),
        out_specs=ANY,
        scratch_shapes=[
            pltpu.VMEM((tok_rows, row_width), jnp.bfloat16),
            pltpu.SemaphoreType.DMA((tok_rows // step,)),
        ],
        compiler_params=PARAMS,
        name="scale_rows",
    )(gain.reshape(1, row_width), *sums, near(attended))


def per_device(queries, keys, values, block_perm, norm_gain):
    sizes = Sizes(queries, block_perm)
    head_size = lax.axis_size("head")
    rank = lax.axis_index("ctx").astype(jnp.int32).reshape(1)
    received = {}

    def exchange(sends):
        for message, array in sends.items():
            route = [(i, i ^ message[0]) for i in range(sizes.ctx)]
            received[message] = lax.ppermute(array, "ctx", route)

    first, steps = schedule(sizes.ctx, sizes.capacity)
    last_block = last_blocks(sizes, keys, values)
    keys, values, sends = first_sends(sizes, first, rank, block_perm, keys, values)
    with jax.named_scope("previous"):
        route = [(i, i + 1) for i in range(sizes.ctx - 1)]
        received["prev"] = lax.ppermute(last_block, "ctx", route)
    exchange(sends)
    queries, state, table, sends = base(
        sizes, steps[0][1], rank, block_perm, queries, keys, values
    )
    exchange(sends)
    for group, partners in steps[1:]:
        last = group == steps[-1][0]
        state, extra = update(
            sizes, group, partners, last, rank, block_perm, table, queries, keys, values,
            received, state,
        )
        exchange(dict(zip(partners, extra)))
    sums = [extra[-1]]
    for d in range(1, head_size):
        sums.append(lax.ppermute(sums[0], "head", [(i, i ^ d) for i in range(head_size)]))
    return scaled(state[0], sums, norm_gain, sizes.width * head_size, sizes.block_len // 2)


def solution(mesh):
    placed = (P("ctx", "head"), P("ctx", "head"), P("ctx", "head"), P("head", None), P("head"))
    return jax.shard_map(
        per_device, mesh=mesh, in_specs=placed, out_specs=P("ctx", "head"), check_vma=False
    )
```

```python
import functools
import math

import jax
import jax.numpy as jnp
from jax import lax
from jax.experimental import pallas as pl
from jax.experimental.pallas import tpu as pltpu
from jax.sharding import PartitionSpec as P

NORM_EPS = 1e-06
ANY = pl.BlockSpec(memory_space=pl.ANY)
SMEM = pl.BlockSpec(memory_space=pltpu.SMEM)
VMEM = pl.BlockSpec(memory_space=pltpu.VMEM)
PARAMS = pltpu.CompilerParams(vmem_limit_bytes=16 * 1024 * 1024)
CONTRACT_LAST = (((1,), (1,)), ((), ()))


class Sizes:
    def __init__(self, queries, block_perm):
        self.ctx = lax.axis_size("ctx")
        self.heads = block_perm.shape[0]
        self.blocks = block_perm.shape[1] // self.ctx
        self.tokens, self.width = queries.shape
        self.block_len = self.tokens // self.blocks
        self.head_dim = self.width // self.heads
        self.capacity = self.heads // 2
        self.full = self.ctx * self.capacity == self.heads * self.blocks
        self.exponent = math.log2(math.e) / math.sqrt(self.head_dim)

    def tile(self, block, head):
        rows = pl.ds(pl.multiple_of(block * self.block_len, self.block_len), self.block_len)
        return rows, pl.ds(pl.multiple_of(head * self.head_dim, self.head_dim), self.head_dim)

    def send_shape(self, message):
        _, low, high = message
        return (2, high - low, self.block_len, self.head_dim)


def schedule(ctx, capacity):
    whole = {d: (d, 0, capacity) for d in range(ctx)}
    if ctx == 8:
        half = capacity // 2
        (five, last_five), (three, last_three) = [
            ((d, 0, half), (d, half, capacity)) for d in (5, 3)
        ]
        steps = [
            ("base", [whole[2]]),
            ("prev", [five]),
            ((whole[0], whole[1]), [three]),
            ((whole[6],), [last_five]),
            ((whole[7],), [last_three]),
            ((whole[4],), []),
            ((whole[2],), []),
            ((five,), []),
            ((three,), []),
            ((last_five,), []),
            ((last_three,), []),
        ]
        return [whole[d] for d in (6, 7, 4, 1)], steps
    rest = [whole[d] for d in range(1, ctx)]
    return rest, [("base", []), ("prev", []), ((whole[0],), [])] + [((m,), []) for m in rest]


def near(array):
    return pltpu.with_memory_space_constraint(array, pltpu.VMEM)


def far(array):
    return pltpu.with_memory_space_constraint(array, pltpu.HBM)


def wanted(sizes, d, rank, perm):
    start = jnp.bitwise_xor(rank, d) * sizes.blocks
    slot = jnp.int32(0)
    for head in range(sizes.heads):
        found = jnp.int32(-1)
        for j in range(sizes.blocks):
            source = perm[head, start + j] - rank * sizes.blocks
            found = jnp.where((source >= 0) & (source < sizes.blocks), source, found)
        yield head, found, slot
        slot = slot + (found >= 0).astype(jnp.int32)


def pack_near(sizes, message, items, which, array, send):
    _, low, high = message
    for head, found, slot in items:
        here = (found >= 0) & (slot >= low) & (slot < high)

        @pl.when(found >= 0 if high - low == sizes.capacity else here)
        def _():
            send[which, slot - low] = array[sizes.tile(found, head)]


def pack_both(sizes, message, rank, perm, keys, values, send):
    items = list(wanted(sizes, message[0], rank, perm))
    for which, array in enumerate((keys, values)):
        pack_near(sizes, message, items, which, array, send)


def last_kernel(block_len, keys, values, last, sems):
    rows = pl.ds(keys.shape[0] - block_len, block_len)
    copies = [
        pltpu.make_async_copy(array.at[rows], last.at[i], sems.at[i])
        for i, array in enumerate((keys, values))
    ]
    for copy in copies:
        copy.start()
    for copy in copies:
        copy.wait()


def last_blocks(sizes, keys, values):
    return pl.pallas_call(
        functools.partial(last_kernel, sizes.block_len),
        out_shape=pltpu.VMEM((2, sizes.block_len, sizes.width), keys.dtype),
        in_specs=[ANY, ANY],
        out_specs=VMEM,
        scratch_shapes=[pltpu.SemaphoreType.DMA((2,))],
        compiler_params=PARAMS,
        cost_estimate=pl.CostEstimate(flops=1, bytes_accessed=1, transcendentals=0),
        name="last_blocks",
    )(far(keys), far(values))


def first_kernel(
    sizes, partners, rank_ref, perm_far, keys, values, near_keys, near_values, *rest
):
    sends, (perm, perm_sem, sems) = rest[:-3], rest[-3:]
    perm_copy = pltpu.make_async_copy(perm_far, perm, perm_sem.at[0])
    perm_copy.start()
    copies = [
        pltpu.make_async_copy(keys, near_keys, sems.at[0]),
        pltpu.make_async_copy(values, near_values, sems.at[1]),
    ]
    for copy in copies:
        copy.start()
    perm_copy.wait()
    found = [list(wanted(sizes, m[0], rank_ref[0], perm)) for m in partners]
    for i, (copy, array) in enumerate(zip(copies, (near_keys, near_values))):
        copy.wait()
        for message, items, send in zip(partners, found, sends):
            pack_near(sizes, message, items, i, array, send)


def first_sends(sizes, partners, rank, perm, keys, values):
    near_keys, near_values, *sends = pl.pallas_call(
        functools.partial(first_kernel, sizes, partners),
        out_shape=[pltpu.VMEM(keys.shape, keys.dtype)] * 2
        + [pltpu.VMEM(sizes.send_shape(m), keys.dtype) for m in partners],
        in_specs=[SMEM, ANY, ANY, ANY],
        out_specs=[VMEM] * (2 + len(partners)),
        scratch_shapes=[
            pltpu.SMEM(perm.shape, perm.dtype),
            pltpu.SemaphoreType.DMA((1,)),
            pltpu.SemaphoreType.DMA((2,)),
        ],
        compiler_params=PARAMS,
        cost_estimate=pl.CostEstimate(flops=1, bytes_accessed=1, transcendentals=0),
        name="first_sends",
    )(rank, far(perm), far(keys), far(values))
    return near_keys, near_values, dict(zip(partners, sends))


def weigh(sizes, scores, peak, values):
    weights = jnp.exp2((scores - peak) * sizes.exponent).astype(jnp.bfloat16)
    ones = jnp.ones(values.shape, values.dtype)
    both = jnp.concatenate([values, ones], axis=1)
    return jnp.dot(weights, both, preferred_element_type=jnp.float32)


def list_matches(sizes, rank, perm, table, counts):
    for d in range(sizes.ctx):
        counts[d] = 0
        if not sizes.full:
            for c in range(sizes.capacity):
                table[d * sizes.capacity + c] = -1
    for head in range(sizes.heads):
        for j in range(sizes.blocks):
            source = perm[head, rank * sizes.blocks + j]
            d = jnp.bitwise_xor(lax.div(source, sizes.blocks), rank)
            slot = counts[d]
            counts[d] = slot + 1
            table[d * sizes.capacity + slot] = (head * sizes.blocks + j) * sizes.blocks + lax.rem(
                source, sizes.blocks
            )


def base_kernel(sizes, partners, rank_ref, perm, queries, keys, values, *rest):
    near_queries, mixture, weight_sum, peaks, squares, table, *sends = rest[: 6 + len(partners)]
    counts, sem = rest[6 + len(partners) :]
    copy = pltpu.make_async_copy(queries, near_queries, sem.at[0])
    copy.start()
    rank = rank_ref[0]
    for message, send in zip(partners, sends):
        pack_both(sizes, message, rank, perm, keys, values, send)
    list_matches(sizes, rank, perm, table, counts)
    squares[...] = jnp.zeros_like(squares)
    copy.wait()
    n = sizes.block_len

    def one_head(head, _):
        columns = sizes.tile(0, head)[1]
        for j in range(sizes.blocks):
            here = slice(j * n, (j + 1) * n), columns
            context = slice(max(j - 1, 0) * n, (j + 1) * n), columns
            scores = lax.dot_general(
                near_queries[here],
                keys[context],
                CONTRACT_LAST,
                preferred_element_type=jnp.float32,
            )
            row = lax.broadcasted_iota(jnp.int32, (n, n), 0)
            column = lax.broadcasted_iota(jnp.int32, (n, n), 1)
            own = jnp.where(row >= column, scores[:, -n:], -jnp.inf)
            scores = own if j == 0 else jnp.concatenate([scores[:, :n], own], axis=1)
            peak = jnp.max(scores, axis=1, keepdims=True)
            total = weigh(sizes, scores, peak, values[context])
            mixture[here] = total[:, : sizes.head_dim]
            weight_sum[here] = total[:, sizes.head_dim :]
            peaks[here] = jnp.broadcast_to(peak, (n, sizes.head_dim))
        return 0

    lax.fori_loop(0, sizes.heads, one_head, 0)


def base(sizes, partners, rank, perm, queries, keys, values):
    state = pltpu.VMEM((sizes.tokens, sizes.width), jnp.float32)
    count = sizes.heads * sizes.blocks
    near_queries, *rest = pl.pallas_call(
        functools.partial(base_kernel, sizes, partners),
        out_shape=[
            pltpu.VMEM(queries.shape, queries.dtype),
            state,
            state,
            state,
            pltpu.VMEM((sizes.tokens, sizes.head_dim), jnp.float32),
            jax.ShapeDtypeStruct((sizes.ctx * sizes.capacity,), jnp.int32),
        ]
        + [pltpu.VMEM(sizes.send_shape(m), keys.dtype) for m in partners],
        in_specs=[SMEM, SMEM, ANY, VMEM, VMEM],
        out_specs=[VMEM] * 5 + [SMEM] + [VMEM] * len(partners),
        scratch_shapes=[
            pltpu.SMEM((sizes.ctx,), jnp.int32),
            pltpu.SemaphoreType.DMA((1,)),
        ],
        compiler_params=PARAMS,
        cost_estimate=pl.CostEstimate(flops=1, bytes_accessed=1, transcendentals=0),
        name="base_items",
    )(rank, perm, far(queries), near(keys), near(values))
    return near_queries, tuple(rest[:4]), rest[4], dict(zip(partners, rest[5:]))


def update_kernel(sizes, group, partners, last, rank_ref, perm, table, queries, keys, values, *rest):
    before = group == "prev"
    remote = ["prev"] if before else [m for m in group if m[0] > 0]
    received, rest = dict(zip(remote, rest)), rest[len(remote) + 4 :]
    mixture, weight_sum, peaks, squares = rest[:4]
    rank = rank_ref[0]
    for message, send in zip(partners, rest[4:]):
        pack_both(sizes, message, rank, perm, keys, values, send)

    def add(here, key_tile, value_tile):
        scores = lax.dot_general(
            queries[here], key_tile, CONTRACT_LAST, preferred_element_type=jnp.float32
        )
        old = peaks[here]
        new = jnp.maximum(old, jnp.max(scores, axis=1, keepdims=True))
        wide = jnp.concatenate([new] * (sizes.block_len // sizes.head_dim), axis=1)
        total = weigh(sizes, scores, wide, value_tile)
        shrink = jnp.exp2((old - new) * sizes.exponent)
        mixed = mixture[here] * shrink + total[:, : sizes.head_dim]
        summed = weight_sum[here] * shrink + total[:, sizes.head_dim :]
        if before:
            mixture[here] = mixed
            weight_sum[here] = summed
            peaks[here] = new
        else:
            attended = mixed / summed
            mixture[here] = attended
            squares[here[0]] += attended * attended

    if before:

        @pl.when(rank > 0)
        def _():
            for head in range(sizes.heads):
                here = sizes.tile(0, head)
                add(here, *[received["prev"][i, :, here[1]] for i in range(2)])

        return

    def match(message, c, item):
        head = lax.div(item, sizes.blocks * sizes.blocks)
        here = sizes.tile(lax.rem(lax.div(item, sizes.blocks), sizes.blocks), head)
        if message[0] > 0:
            add(here, *[received[message][i, c - message[1]] for i in range(2)])
        else:
            there = sizes.tile(lax.rem(item, sizes.blocks), head)
            add(here, keys[there], values[there])

    for message in group:
        d, low, high = message
        for c in range(low, high):
            item = table[d * sizes.capacity + c]
            if sizes.full:
                match(message, c, item)
            else:
                pl.when(item >= 0)(functools.partial(match, message, c, item))
    if last:
        ones = jnp.ones((8, sizes.head_dim), jnp.bfloat16)
        rest_of = squares[...]
        total = None
        for _ in range(3):
            part = rest_of.astype(jnp.bfloat16)
            rest_of = rest_of - part.astype(jnp.float32)
            summed = lax.dot_general(ones, part, CONTRACT_LAST, preferred_element_type=jnp.float32)
            total = summed if total is None else total + summed
        rest[4][...] = total[:1]


def update(sizes, group, partners, last, rank, perm, table, queries, keys, values, received, state):
    remote = ["prev"] if group == "prev" else [m for m in group if m[0] > 0]
    remote = [received[m] for m in remote]
    arrays = [near(a) for a in [queries, keys, values] + remote + list(state)]
    out_shape = [pltpu.VMEM(a.shape, a.dtype) for a in state]
    out_shape += [pltpu.VMEM(sizes.send_shape(m), keys.dtype) for m in partners]
    if last:
        out_shape.append(jax.ShapeDtypeStruct((1, sizes.tokens), jnp.float32))
    first_state = 3 + len(arrays) - len(state)
    out = pl.pallas_call(
        functools.partial(update_kernel, sizes, group, partners, last),
        out_shape=out_shape,
        in_specs=[SMEM] * 3 + [VMEM] * len(arrays),
        out_specs=[VMEM] * len(out_shape),
        input_output_aliases={first_state + i: i for i in range(len(state))},
        compiler_params=PARAMS,
        cost_estimate=pl.CostEstimate(flops=1, bytes_accessed=1, transcendentals=0),
        name="update_items",
    )(rank, perm, table, *arrays)
    return tuple(out[:4]), out[4:]


def scale_kernel(width, step, gain, *rest):
    sums, (attended, out, buffer, sems) = rest[:-4], rest[-4:]
    total = sums[0][...]
    for other in sums[1:]:
        total = total + other[...]
    inverse = lax.rsqrt(total / width + NORM_EPS)
    steps = attended.shape[0] // step
    copies = []
    for i in range(steps):
        rows = slice(i * step, (i + 1) * step)
        column = jnp.transpose(jnp.broadcast_to(inverse[:, rows], (8, step)))[:, :1]
        buffer[rows] = (attended[rows] * column * gain[...]).astype(out.dtype)
        copies.append(pltpu.make_async_copy(buffer.at[rows], out.at[rows], sems.at[i]))
        copies[i].start()
    for copy in copies:
        copy.wait()


def scaled(attended, sums, gain, width, step):
    tok_rows, row_width = attended.shape
    return pl.pallas_call(
        functools.partial(scale_kernel, width, step),
        out_shape=jax.ShapeDtypeStruct((tok_rows, row_width), jnp.bfloat16),
        in_specs=[VMEM] * (len(sums) + 2),
        out_specs=ANY,
        scratch_shapes=[
            pltpu.VMEM((tok_rows, row_width), jnp.bfloat16),
            pltpu.SemaphoreType.DMA((tok_rows // step,)),
        ],
        compiler_params=PARAMS,
        name="scale_rows",
    )(gain.reshape(1, row_width), *sums, near(attended))


def per_device(queries, keys, values, block_perm, norm_gain):
    sizes = Sizes(queries, block_perm)
    head_size = lax.axis_size("head")
    rank = lax.axis_index("ctx").astype(jnp.int32).reshape(1)
    received = {}

    def exchange(sends):
        for message, array in sends.items():
            route = [(i, i ^ message[0]) for i in range(sizes.ctx)]
            received[message] = lax.ppermute(array, "ctx", route)

    first, steps = schedule(sizes.ctx, sizes.capacity)
    last_block = last_blocks(sizes, keys, values)
    keys, values, sends = first_sends(sizes, first, rank, block_perm, keys, values)
    with jax.named_scope("previous"):
        route = [(i, i + 1) for i in range(sizes.ctx - 1)]
        received["prev"] = lax.ppermute(last_block, "ctx", route)
    exchange(sends)
    queries, state, table, sends = base(
        sizes, steps[0][1], rank, block_perm, queries, keys, values
    )
    exchange(sends)
    for group, partners in steps[1:]:
        last = group == steps[-1][0]
        state, extra = update(
            sizes, group, partners, last, rank, block_perm, table, queries, keys, values,
            received, state,
        )
        exchange(dict(zip(partners, extra)))
    sums = [extra[-1]]
    for d in sorted(range(1, head_size), key=lambda d: (d % 2 == 0, d)):
        sums.append(lax.ppermute(sums[0], "head", [(i, i ^ d) for i in range(head_size)]))
    return scaled(state[0], sums, norm_gain, sizes.width * head_size, sizes.block_len // 2)


def solution(mesh):
    placed = (P("ctx", "head"), P("ctx", "head"), P("ctx", "head"), P("head", None), P("head"))
    return jax.shard_map(
        per_device, mesh=mesh, in_specs=placed, out_specs=P("ctx", "head"), check_vma=False
    )
```
